256 devices in a mesh: sec: 16 (over z, core), op: 16 (over x, y).
Axes of the slice: x: 4, y: 4, z: 8, core: 2. Of those that a mesh axis runs over, the one named last changes fastest.
Arguments:
- theta: float32 [32, 512, 512], P('sec', 'op'), may hold values from -6 to 6
- counts: int32 [32], P('sec'), may hold values from 256 to 512, as said below
- pair_source: int32 [256], P('sec'), may hold values from 0 to 1
- pair_target: int32 [256], P('sec'), may hold values from 0 to 31
- left_ops: float32 [1024, 512, 512], P(('sec', 'op')), may hold values from -0.25 to 0.25
- right_ops: float32 [1024, 512, 512], P(('sec', 'op')), may hold values from -0.25 to 0.25
Outputs:
- cheb_last: float32 [32, 512, 512], P('sec', 'op')
- cheb_prev: float32 [32, 512, 512], P('sec', 'op')
The draws below stay inside these ranges and needn't reach their ends.
Inputs may be any that keep to these rules, and one draw needn't show every extreme that they name: `counts`: every sector has between 256 and 512 live states; some sector has exactly 512 and some exactly 256.
All inputs are finite; a program needn't handle non-finite values.
Results may differ from the reference program's by a relative error of at most 0.0001.
Values sent between devices are 32-bit elements; how exact they have to be, the bound alone decides.
A program may use at most 64 MiB of HBM per device.

```python
import math
import jax
import jax.numpy as jnp
from jax import lax

M = 512
SEC_DEV = 2
PAIRS_DEV = 4
STEPS = 3
SECTORS = 32
BLOCKS = 256
PAIRS = 1024
N_OP = 16


def draw_counts(key, part):
    base_counts = jax.random.randint(jax.random.fold_in(key, 11), (SECTORS,), M // 2, M + 1)
    full_place = jax.random.randint(jax.random.fold_in(key, 12), (), 0, SECTORS)
    offset = jax.random.randint(jax.random.fold_in(key, 13), (), 1, SECTORS)
    small_place = (full_place + offset) % SECTORS
    base_counts = base_counts.at[full_place].set(M)
    base_counts = base_counts.at[small_place].set(M // 2)
    return base_counts.astype(jnp.int32)


def place_ends(entries, stream_key, least, high):
    longest = entries.shape.index(max(entries.shape))
    spots = []
    for shift in (0, 1):
        where = [jax.random.randint(jax.random.fold_in(stream_key, axis), (), 0, length) for axis, length in enumerate(entries.shape)]
        where[longest] = (where[longest] + shift) % entries.shape[longest]
        spots.append(tuple(where))
    return entries.at[spots[0]].set(least).at[spots[1]].set(high)


def block_scale(key, dims, cuts, smallest, largest):
    gain, own = 1.0, jax.random.fold_in(key, 6)
    for dim, blocks in cuts:
        steps = jnp.exp(jax.random.uniform(jax.random.fold_in(own, dim), (blocks,), jnp.float32, smallest / len(cuts), largest / len(cuts)))
        gain = gain * jnp.repeat(steps, dims[dim] // blocks).reshape([-1 if axis == dim else 1 for axis in range(len(dims))])
    return gain


def normal_values(own_key, extent, width, bound, pieces=(), kind=jnp.bfloat16):
    drawn = jax.random.normal(own_key, extent, jnp.float32) * width
    if len(pieces) > 0:
        drawn = block_scale(own_key, extent, pieces, -0.22, 0.18) * drawn
    return jnp.clip(drawn, min=-bound, max=bound).astype(kind)


def setup_inputs(seed: int = 0) -> dict:
    arg_keys = jax.random.split(jax.random.key(seed), 7)
    return {
        "theta": normal_values(arg_keys[0], (SECTORS, M, M), 1.0, 6.0, ((0, 16), (1, 16)), jnp.float32),
        "counts": draw_counts(jax.random.fold_in(arg_keys[6], 71), 0),
        "pair_source": place_ends(jax.random.randint(arg_keys[2], (BLOCKS,), 0, SEC_DEV), jax.random.fold_in(arg_keys[2], 1), 0, SEC_DEV - 1).astype(jnp.int32),
        "pair_target": place_ends(jax.random.randint(arg_keys[3], (BLOCKS,), 0, SECTORS), jax.random.fold_in(arg_keys[3], 1), 0, SECTORS - 1).astype(jnp.int32),
        "left_ops": normal_values(arg_keys[4], (PAIRS, M, M), M ** -0.5, 0.25, ((0, 256),), jnp.float32),
        "right_ops": normal_values(arg_keys[5], (PAIRS, M, M), M ** -0.5, 0.25, ((0, 256),), jnp.float32),
    }


def sector_live(counts):
    positions = jnp.arange(M, dtype=jnp.int32)
    alive = positions[None, :] < counts[:, None]
    return alive[:, :, None] & alive[:, None, :]

def apply_hamiltonian(iterate, live_mask, source_global, pair_target, left_ops, right_ops, factor):

    def add_pair(running, pair_item):
        source, target, left_op, right_op = pair_item
        sector_block = lax.dynamic_index_in_dim(iterate, source, 0, keepdims=False)
        left_product = jnp.dot(left_op, sector_block, precision=lax.Precision.HIGHEST)
        pair_term = jnp.dot(left_product, right_op.T, precision=lax.Precision.HIGHEST)
        return (running.at[target].add(pair_term), None)
    summed, _ = lax.scan(add_pair, jnp.zeros_like(iterate), (source_global, pair_target, left_ops, right_ops))
    return factor * jnp.where(live_mask, summed, jnp.zeros_like(summed))

def reference(theta, counts, pair_source, pair_target, left_ops, right_ops):
    live_mask = sector_live(counts)
    block_of_pair = (jnp.arange(PAIRS, dtype=jnp.int32) // PAIRS_DEV).astype(jnp.int32)
    group_of_block = (jnp.arange(BLOCKS, dtype=jnp.int32) // N_OP).astype(jnp.int32)
    block_source = (group_of_block * SEC_DEV + pair_source).astype(jnp.int32)
    source_global = block_source[block_of_pair].astype(jnp.int32)
    target_global = pair_target[block_of_pair].astype(jnp.int32)
    factor = 0.5 / math.sqrt(N_OP * PAIRS_DEV / SEC_DEV)
    previous = jnp.where(live_mask, theta, jnp.zeros_like(theta))
    current = apply_hamiltonian(previous, live_mask, source_global, target_global, left_ops, right_ops, factor)
    for step_number in range(STEPS - 1):
        following = 2.0 * apply_hamiltonian(current, live_mask, source_global, target_global, left_ops, right_ops, factor) - previous
        previous, current = (current, following)
    return (current, previous)
```

```python
import functools
import math

import jax
import jax.numpy as jnp
from jax import lax
from jax.experimental import pallas as pl
from jax.experimental.pallas import tpu as pltpu
from jax.sharding import PartitionSpec as P

STEPS = 3
CHUNKS = 4
HOPS = 4
MESH = pl.DeviceIdType.MESH
F32 = jnp.float32
BF16 = jnp.bfloat16
NT = (((1,), (1,)), ((), ()))


def split(value):
    high = value.astype(BF16)
    return high, (value - high.astype(F32)).astype(BF16)


def kernel(
    factor,
    theta, counts, source, target, left, right,
    last_out, prev_out,
    left_raw, right_raw, left_hi, left_lo, right_two, x_hi, x_lo,
    current, previous, chosen, gathered, terms, arrived, running,
    pass_out, pass_in, sums, ring_in,
    before, final,
    load_sem, gather_send, gather_recv, rows_send, rows_recv,
    pass_send, pass_recv, ring_send, ring_recv,
):
    sec, op = lax.axis_index("sec"), lax.axis_index("op")
    z, core = sec // 2, sec % 2
    op_x, op_y = op // 4, op % 4
    size = left.shape[1]
    pairs = left.shape[0]
    width = size // CHUNKS
    rows = theta.shape[1]
    blocks = target.shape[0]
    sectors = final.shape[0]

    load_left = pltpu.make_async_copy(left, left_raw, load_sem.at[0])
    load_right = pltpu.make_async_copy(right, right_raw, load_sem.at[1])
    load_left.start()
    load_right.start()

    def op_peer(k):
        return ((op_x + k // 4) % 4) * 4 + (op_y + k % 4) % 4

    barrier = pltpu.get_barrier_semaphore()

    @pl.loop(1, blocks)
    def _(k):
        pl.semaphore_signal(barrier, 1, device_id=(sec, op_peer(k)), device_id_type=MESH)

    for other in (z * 2 + (core + 1) % 2, ((z + 1) % 8) * 2 + core, ((z + 7) % 8) * 2 + core):
        pl.semaphore_signal(barrier, 1, device_id=(other, op), device_id_type=MESH)

    def live(h, c):
        row = lax.broadcasted_iota(jnp.int32, (rows, width), 0) + op * rows
        column = lax.broadcasted_iota(jnp.int32, (rows, width), 1) + c * width
        return (row < counts[h]) & (column < counts[h])

    def gather_start(c):
        first, second = current[c, 0], current[c, 1]
        for j in range(blocks):
            chosen[c, j] = jnp.where(source[j] == 0, first, second)
        pltpu.make_async_copy(chosen.at[c, op], gathered.at[c, op], gather_recv.at[c]).start()

        @pl.loop(1, blocks)
        def _(k):
            peer = op_peer(k)
            pltpu.make_async_remote_copy(
                chosen.at[c, peer], gathered.at[c, op], gather_send.at[c], gather_recv.at[c],
                device_id=(sec, peer), device_id_type=MESH,
            ).start()

    def wait_for(ref, sem):
        pltpu.make_async_copy(ref, ref, sem).wait()

    for c in range(CHUNKS):
        for h in range(2):
            piece = theta[h, :, c * width : (c + 1) * width]
            current[c, h] = jnp.where(live(h, c), piece, 0.0)
    previous[...] = jnp.zeros_like(previous)
    running[blocks] = jnp.zeros((rows, width), F32)

    pl.semaphore_wait(barrier, blocks - 1 + 3)

    @pl.loop(0, CHUNKS)
    def _(c):
        gather_start(c)

    for b in range(blocks):
        found = jnp.int32(blocks)
        for a in range(b):
            found = jnp.where(target[a] == target[b], a, found)
        before[b] = found

    @pl.loop(0, sectors)
    def _(q):
        found = jnp.int32(blocks)
        for b in range(blocks):
            found = jnp.where(target[b] == q, b, found)
        final[q] = found

    load_left.wait()

    @pl.loop(0, pairs * size // 128)
    def _(i):
        p, r = i // (size // 128), pl.multiple_of((i % (size // 128)) * 128, 128)
        at = pl.multiple_of(i * 128, 128)
        high, low = split(left_raw[p, pl.ds(r, 128), :])
        left_hi[pl.ds(at, 128), :] = high
        left_lo[pl.ds(at, 128), :] = low

    load_right.wait()

    @pl.loop(0, CHUNKS)
    def _(c):
        for p in range(pairs):
            high, low = split(right_raw[p, pl.ds(pl.multiple_of(c * width, width), width), :])
            right_two[c, 0:width, p * size : (p + 1) * size] = high
            right_two[c, width : 2 * width, p * size : (p + 1) * size] = low

    def rows_start(c):
        pltpu.make_async_copy(terms.at[c, op], arrived.at[c, op], rows_recv.at[c]).start()

        @pl.loop(1, blocks)
        def _(k):
            peer = op_peer(k)
            pltpu.make_async_remote_copy(
                terms.at[c, peer], arrived.at[c, op], rows_send.at[c], rows_recv.at[c],
                device_id=(sec, peer), device_id_type=MESH,
            ).start()

    def ring_start(side, h, c, j, dest):
        near = ((z + 1 + 6 * side) % 8) * 2 + core
        pltpu.make_async_remote_copy(
            sums.at[c, dest], ring_in.at[h, side, j - 1, c], ring_send.at[c],
            ring_recv.at[h, side, j - 1, c],
            device_id=(near, op), device_id_type=MESH,
        ).start()

    def ring_dest(side, j):
        return (z + (5 - j) * (1 - side) + (3 + j) * side) % 8

    def ring_wait(side, h, j, c):
        wait_for(ring_in.at[h, side, j - 1, c], ring_recv.at[h, side, j - 1, c])

    def step(k):
        half = k % 2

        @pl.loop(0, CHUNKS)
        def _(c):
            wait_for(gathered.at[c], gather_recv.at[c])
            high, low = split(gathered[c].reshape(size, width))
            both = jnp.concatenate([high, low], axis=1)
            lane = pl.multiple_of(c * width, width)

            @pl.loop(0, pairs)
            def _(p):
                at = pl.multiple_of(p * size, size)
                a = jnp.dot(left_hi[pl.ds(at, size), :], both, preferred_element_type=F32)
                b = jnp.dot(left_lo[pl.ds(at, size), :], high, preferred_element_type=F32)
                x_high, x_low = split(a[:, :width] + a[:, width:] + b)
                x_hi[:, pl.ds(at + lane, width)] = x_high
                x_lo[:, pl.ds(at + lane, width)] = x_low

        @pl.loop(0, CHUNKS)
        def _(c):
            wait_for(gathered.at[c, 0 : blocks - 1], gather_send.at[c])

        @pl.loop(0, CHUNKS)
        def _(c):
            both, high = right_two[c], right_two[c, 0:width, :]
            for part in range(2):
                r = part * (size // 2)
                a = lax.dot_general(x_hi[r : r + size // 2, :], both, NT, preferred_element_type=F32)
                b = lax.dot_general(x_lo[r : r + size // 2, :], high, NT, preferred_element_type=F32)
                block_rows = a[:, :width] + a[:, width:] + b
                terms[c, part * (blocks // 2) : (part + 1) * (blocks // 2)] = block_rows.reshape(
                    blocks // 2, rows, width
                )
            rows_start(c)

        def sum_blocks(c):
            wait_for(arrived.at[c], rows_recv.at[c])
            for b in range(blocks):
                running[b] = arrived[c, b] + running[before[b]]
            for there in range(8):
                for h in range(2):
                    pass_out[c, there, h] = running[final[4 * there + 2 * (1 - core) + h]]
                    sums[c, there, h] = running[final[4 * there + 2 * core + h]]
            pltpu.make_async_remote_copy(
                pass_out.at[c], pass_in.at[half, c], pass_send.at[c], pass_recv.at[half, c],
                device_id=(z * 2 + (core + 1) % 2, op), device_id_type=MESH,
            ).start()

        def ring_first(c):
            wait_for(pass_in.at[half, c], pass_recv.at[half, c])
            sums[c] = sums[c] + pass_in[half, c]
            side = c % 2
            ring_start(side, half, c, 1, ring_dest(side, 1))

        def ring_second(c):
            side = c % 2
            other = 1 - side
            ring_start(other, half, c, 2, ring_dest(other, 2))
            ring_wait(side, half, 1, c)
            dest = ring_dest(side, 2)
            sums[c, dest] = sums[c, dest] + ring_in[half, side, 0, c]
            ring_start(side, half, c, 2, dest)

        def ring_next(c, j):
            for side in range(2):
                ring_wait(side, half, j - 1, c)
                dest = ring_dest(side, j)
                sums[c, dest] = sums[c, dest] + ring_in[half, side, j - 2, c]
                ring_start(side, half, c, j, dest)

        def finish(c):
            ring_wait(0, half, HOPS, c)
            ring_wait(1, half, HOPS, c)
            scale = jnp.where(k == 0, factor, 2.0 * factor).astype(F32)
            keep = jnp.where(k == 0, 0.0, 1.0).astype(F32)
            for h in range(2):
                total = sums[c, z, h] + ring_in[half, 0, HOPS - 1, c, h] + ring_in[half, 1, HOPS - 1, c, h]
                following = jnp.where(live(h, c), scale * total, 0.0) - keep * previous[c, h]
                previous[c, h] = current[c, h]
                current[c, h] = following

            @pl.when(k < STEPS - 1)
            def _():
                gather_start(c)

        stages = [
            sum_blocks, ring_first, ring_second,
            lambda c: ring_next(c, 3), lambda c: ring_next(c, 4), finish,
        ]

        @pl.loop(0, CHUNKS + len(stages) - 1)
        def _(t):
            for s in reversed(range(len(stages))):
                c = t - s

                @pl.when((c >= 0) & (c < CHUNKS))
                def _():
                    stages[s](c)

        @pl.loop(0, CHUNKS)
        def _(c):
            wait_for(arrived.at[c, 0 : blocks - 1], rows_send.at[c])
            wait_for(pass_out.at[c], pass_send.at[c])
            wait_for(sums.at[c, 0:7], ring_send.at[c])

    pl.loop(0, STEPS)(step)

    for c in range(CHUNKS):
        for h in range(2):
            last_out[h, :, c * width : (c + 1) * width] = current[c, h]
            prev_out[h, :, c * width : (c + 1) * width] = previous[c, h]


def per_device(theta, counts, pair_source, pair_target, left_ops, right_ops):
    sec_local, rows, size = theta.shape
    pairs = left_ops.shape[0]
    blocks = pair_target.shape[0]
    sectors = sec_local * lax.axis_size("sec")
    places = sectors // (2 * sec_local)
    factor = 0.5 / math.sqrt(blocks * pairs / sec_local)
    width = size // CHUNKS
    vmem, smem = pltpu.VMEM, pltpu.SMEM
    tile = (rows, width)
    flops = STEPS * pairs * 2 * 2 * 3 * size**3
    return pl.pallas_call(
        functools.partial(kernel, factor),
        out_shape=[jax.ShapeDtypeStruct(theta.shape, F32)] * 2,
        in_specs=[pl.BlockSpec(memory_space=vmem)]
        + [pl.BlockSpec(memory_space=smem)] * 3
        + [pl.BlockSpec(memory_space=pl.ANY)] * 2,
        out_specs=[pl.BlockSpec(memory_space=vmem)] * 2,
        scratch_shapes=[
            vmem(left_ops.shape, F32),
            vmem(left_ops.shape, F32),
            vmem((pairs * size, size), BF16),
            vmem((pairs * size, size), BF16),
            vmem((CHUNKS, 2 * width, pairs * size), BF16),
            vmem((size, pairs * size), BF16),
            vmem((size, pairs * size), BF16),
            vmem((CHUNKS, sec_local) + tile, F32),
            vmem((CHUNKS, sec_local) + tile, F32),
            vmem((CHUNKS, blocks) + tile, F32),
            vmem((CHUNKS, blocks) + tile, F32),
            vmem((CHUNKS, blocks) + tile, F32),
            vmem((CHUNKS, blocks) + tile, F32),
            vmem((blocks + 1,) + tile, F32),
            vmem((CHUNKS, places, sec_local) + tile, F32),
            vmem((2, CHUNKS, places, sec_local) + tile, F32),
            vmem((CHUNKS, places, sec_local) + tile, F32),
            vmem((2, 2, HOPS, CHUNKS, sec_local) + tile, F32),
            smem((blocks,), jnp.int32),
            smem((sectors,), jnp.int32),
            pltpu.SemaphoreType.DMA((2,)),
            pltpu.SemaphoreType.DMA((CHUNKS,)),
            pltpu.SemaphoreType.DMA((CHUNKS,)),
            pltpu.SemaphoreType.DMA((CHUNKS,)),
            pltpu.SemaphoreType.DMA((CHUNKS,)),
            pltpu.SemaphoreType.DMA((CHUNKS,)),
            pltpu.SemaphoreType.DMA((2, CHUNKS)),
            pltpu.SemaphoreType.DMA((CHUNKS,)),
            pltpu.SemaphoreType.DMA((2, 2, HOPS, CHUNKS)),
        ],
        compiler_params=pltpu.CompilerParams(
            collective_id=0, has_side_effects=True, vmem_limit_bytes=56 * 1024 * 1024
        ),
        cost_estimate=pl.CostEstimate(
            flops=flops, bytes_accessed=8 * left_ops.size, transcendentals=0
        ),
    )(theta, counts, pair_source, pair_target, left_ops, right_ops)


def solution(mesh):
    in_specs = (
        P("sec", "op", None),
        P("sec"),
        P("sec"),
        P("sec"),
        P(("sec", "op"), None, None),
        P(("sec", "op"), None, None),
    )
    out_specs = (P("sec", "op", None), P("sec", "op", None))
    return jax.shard_map(
        per_device, mesh=mesh, in_specs=in_specs, out_specs=out_specs, check_vma=False
    )
```

```python
import functools
import math

import jax
import jax.numpy as jnp
from jax import lax
from jax.experimental import pallas as pl
from jax.experimental.pallas import tpu as pltpu
from jax.sharding import PartitionSpec as P

STEPS = 3
CHUNKS = 4
CUTS = 2
PARTS = CHUNKS * CUTS
SLOTS = 4
PACE = 1
FIRST_AT, HUB_AT, FINISH_AT = 1, 4, 7
MESH = pl.DeviceIdType.MESH
F32 = jnp.float32
BF16 = jnp.bfloat16
NT = (((1,), (1,)), ((), ()))


def split(value):
    high = value.astype(BF16)
    return high, (value - high.astype(F32)).astype(BF16)


def kernel(
    factor,
    theta, counts, source, target, left, right,
    last_out, prev_out,
    left_raw, right_raw, left_hi, left_lo, right_two, x_hi, x_lo,
    current, previous, chosen, gathered, terms, arrived, running,
    pass_out, pass_in, sums, sums_in,
    before, final,
    load_sem, gather_send, gather_recv, rows_send, rows_recv,
    pass_send, pass_recv, sums_send, sums_recv,
):
    sec, op = lax.axis_index("sec"), lax.axis_index("op")
    z, core = sec // 2, sec % 2
    op_x, op_y = op // 4, op % 4
    size = left.shape[1]
    pairs = left.shape[0]
    width = size // CHUNKS
    rows = theta.shape[1]
    cut = rows // CUTS
    blocks = target.shape[0]
    sectors = final.shape[0]

    load_left = pltpu.make_async_copy(left, left_raw, load_sem.at[0])
    load_right = pltpu.make_async_copy(right, right_raw, load_sem.at[1])
    load_left.start()
    load_right.start()

    def op_peer(k):
        return ((op_x + k // 4) % 4) * 4 + (op_y + k % 4) % 4

    barrier = pltpu.get_barrier_semaphore()

    @pl.loop(1, blocks)
    def _(k):
        pl.semaphore_signal(barrier, 1, device_id=(sec, op_peer(k)), device_id_type=MESH)

    pl.semaphore_signal(barrier, 1, device_id=(z * 2 + (core + 1) % 2, op), device_id_type=MESH)
    for away in (1, 2, 6, 7):
        other = ((z + away) % 8) * 2 + core
        pl.semaphore_signal(barrier, 1, device_id=(other, op), device_id_type=MESH)

    def place(e):
        return e // CUTS, pl.ds(pl.multiple_of((e % CUTS) * cut, cut), cut)

    def live(h, e):
        row = lax.broadcasted_iota(jnp.int32, (cut, width), 0) + (op * rows + (e % CUTS) * cut)
        column = lax.broadcasted_iota(jnp.int32, (cut, width), 1) + (e // CUTS) * width
        return (row < counts[h]) & (column < counts[h])

    def gather_start(e):
        c, part = place(e)
        first, second = current[e, 0], current[e, 1]
        for j in range(blocks):
            chosen[e, j] = jnp.where(source[j] == 0, first, second)
        pltpu.make_async_copy(chosen.at[e, op], gathered.at[c, op, part], gather_recv.at[e]).start()

        @pl.loop(1, blocks)
        def _(k):
            peer = op_peer(k)
            pltpu.make_async_remote_copy(
                chosen.at[e, peer], gathered.at[c, op, part], gather_send.at[e], gather_recv.at[e],
                device_id=(sec, peer), device_id_type=MESH,
            ).start()

    def wait_for(ref, sem):
        pltpu.make_async_copy(ref, ref, sem).wait()

    for e in range(PARTS):
        c, r = e // CUTS, (e % CUTS) * cut
        for h in range(2):
            piece = theta[h, r : r + cut, c * width : (c + 1) * width]
            current[e, h] = jnp.where(live(h, e), piece, 0.0)
    previous[...] = jnp.zeros_like(previous)
    running[blocks] = jnp.zeros((cut, width), F32)

    pl.semaphore_wait(barrier, blocks - 1 + 5)

    @pl.loop(0, PARTS)
    def _(e):
        gather_start(e)

    for b in range(blocks):
        found = jnp.int32(blocks)
        for a in range(b):
            found = jnp.where(target[a] == target[b], a, found)
        before[b] = found

    @pl.loop(0, sectors)
    def _(q):
        found = jnp.int32(blocks)
        for b in range(blocks):
            found = jnp.where(target[b] == q, b, found)
        final[q] = found

    load_left.wait()

    @pl.loop(0, pairs * size // 128)
    def _(i):
        p, r = i // (size // 128), pl.multiple_of((i % (size // 128)) * 128, 128)
        at = pl.multiple_of(i * 128, 128)
        high, low = split(left_raw[p, pl.ds(r, 128), :])
        left_hi[pl.ds(at, 128), :] = high
        left_lo[pl.ds(at, 128), :] = low

    load_right.wait()

    @pl.loop(0, CHUNKS)
    def _(c):
        for p in range(pairs):
            high, low = split(right_raw[p, pl.ds(pl.multiple_of(c * width, width), width), :])
            right_two[c, 0:width, p * size : (p + 1) * size] = high
            right_two[c, width : 2 * width, p * size : (p + 1) * size] = low

    def rows_start(e):
        c, part = place(e)
        pltpu.make_async_copy(terms.at[c, op, part], arrived.at[e, op], rows_recv.at[e]).start()

        @pl.loop(1, blocks)
        def _(k):
            peer = op_peer(k)
            pltpu.make_async_remote_copy(
                terms.at[c, peer, part], arrived.at[e, op], rows_send.at[e], rows_recv.at[e],
                device_id=(sec, peer), device_id_type=MESH,
            ).start()

    def away(side, distance):
        return (z + distance + side * (8 - 2 * distance)) % 8

    def sums_start(side, h, e, slot, dest, distance):
        pltpu.make_async_remote_copy(
            sums.at[e, away(side, dest)], sums_in.at[h, side, slot, e], sums_send.at[e],
            sums_recv.at[h, side, slot, e],
            device_id=(away(side, distance) * 2 + core, op), device_id_type=MESH,
        ).start()

    def sums_wait(side, h, slot, e):
        wait_for(sums_in.at[h, side, slot, e], sums_recv.at[h, side, slot, e])

    def step(k):
        half = k % 2

        @pl.loop(0, CHUNKS)
        def _(c):
            for r in range(CUTS):
                e = c * CUTS + r
                wait_for(chosen.at[e], gather_recv.at[e])
            high, low = split(gathered[c].reshape(size, width))
            both = jnp.concatenate([high, low], axis=1)
            lane = pl.multiple_of(c * width, width)

            @pl.loop(0, pairs)
            def _(p):
                at = pl.multiple_of(p * size, size)
                a = jnp.dot(left_hi[pl.ds(at, size), :], both, preferred_element_type=F32)
                b = jnp.dot(left_lo[pl.ds(at, size), :], high, preferred_element_type=F32)
                x_high, x_low = split(a[:, :width] + a[:, width:] + b)
                x_hi[:, pl.ds(at + lane, width)] = x_high
                x_lo[:, pl.ds(at + lane, width)] = x_low

        @pl.loop(0, PARTS)
        def _(e):
            wait_for(chosen.at[e, 0 : blocks - 1], gather_send.at[e])

        @pl.loop(0, CHUNKS)
        def _(c):
            both, high = right_two[c], right_two[c, 0:width, :]
            for part in range(2):
                r = part * (size // 2)
                a = lax.dot_general(x_hi[r : r + size // 2, :], both, NT, preferred_element_type=F32)
                b = lax.dot_general(x_lo[r : r + size // 2, :], high, NT, preferred_element_type=F32)
                block_rows = a[:, :width] + a[:, width:] + b
                terms[c, part * (blocks // 2) : (part + 1) * (blocks // 2)] = block_rows.reshape(
                    blocks // 2, rows, width
                )
            for r in range(CUTS):
                rows_start(c * CUTS + r)

        def sum_blocks(e):
            wait_for(arrived.at[e], rows_recv.at[e])
            for b in range(blocks):
                running[b] = arrived[e, b] + running[before[b]]
            for there in range(8):
                for h in range(2):
                    pass_out[e, there, h] = running[final[4 * there + 2 * (1 - core) + h]]
            pltpu.make_async_remote_copy(
                pass_out.at[e], pass_in.at[half, e], pass_send.at[e], pass_recv.at[half, e],
                device_id=(z * 2 + (core + 1) % 2, op), device_id_type=MESH,
            ).start()
            for there in range(8):
                for h in range(2):
                    sums[e, there, h] = running[final[4 * there + 2 * core + h]]

        def sums_first(e):
            wait_for(pass_in.at[half, e], pass_recv.at[half, e])
            sums[e] = sums[e] + pass_in[half, e]
            sums_start(e % 2, half, e, 1, 4, 2)
            for side in range(2):
                sums_start(side, half, e, 0, 3, 1)
            for side in range(2):
                sums_start(side, half, e, 2, 1, 1)

        def sums_hub(e):
            for far in range(2):
                side = (e + 1 + far) % 2
                dest = away(side, 2)
                sums_wait(side, half, 0, e)
                total = sums[e, dest] + sums_in[half, side, 0, e]
                if far:
                    sums_wait(side, half, 1, e)
                    total = total + sums_in[half, side, 1, e]
                sums[e, dest] = total
                sums_start(side, half, e, 3, 2, 2)

        def finish(e):
            for side in range(2):
                sums_wait(side, half, 2, e)
                sums_wait(side, half, 3, e)
            scale = jnp.where(k == 0, factor, 2.0 * factor).astype(F32)
            keep = jnp.where(k == 0, 0.0, 1.0).astype(F32)
            for h in range(2):
                near = sums_in[half, 0, 2, e, h] + sums_in[half, 1, 2, e, h]
                far = sums_in[half, 0, 3, e, h] + sums_in[half, 1, 3, e, h]
                total = sums[e, z, h] + (near + far)
                following = jnp.where(live(h, e), scale * total, 0.0) - keep * previous[e, h]
                previous[e, h] = current[e, h]
                current[e, h] = following

            @pl.when(k < STEPS - 1)
            def _():
                gather_start(e)

        @pl.loop(0, (PARTS - 1) * PACE + FINISH_AT + 1)
        def _(t):
            def due(after, stage):
                wave = t - after
                e = wave // PACE

                @pl.when((wave >= 0) & (e < PARTS) & (wave % PACE == 0))
                def _():
                    stage(e)

            due(FINISH_AT, finish)
            due(HUB_AT, sums_hub)
            due(FIRST_AT, sums_first)
            due(0, sum_blocks)

        @pl.loop(0, PARTS)
        def _(e):
            wait_for(arrived.at[e, 0 : blocks - 1], rows_send.at[e])
            wait_for(pass_out.at[e], pass_send.at[e])
            wait_for(sums.at[e, 0:7], sums_send.at[e])

    pl.loop(0, STEPS)(step)

    for e in range(PARTS):
        c, r = e // CUTS, (e % CUTS) * cut
        for h in range(2):
            last_out[h, r : r + cut, c * width : (c + 1) * width] = current[e, h]
            prev_out[h, r : r + cut, c * width : (c + 1) * width] = previous[e, h]


def per_device(theta, counts, pair_source, pair_target, left_ops, right_ops):
    sec_local, rows, size = theta.shape
    pairs = left_ops.shape[0]
    blocks = pair_target.shape[0]
    sectors = sec_local * lax.axis_size("sec")
    places = sectors // (2 * sec_local)
    factor = 0.5 / math.sqrt(blocks * pairs / sec_local)
    width = size // CHUNKS
    vmem, smem = pltpu.VMEM, pltpu.SMEM
    tile = (rows // CUTS, width)
    flops = STEPS * pairs * 2 * 2 * 3 * size**3
    return pl.pallas_call(
        functools.partial(kernel, factor),
        out_shape=[jax.ShapeDtypeStruct(theta.shape, F32)] * 2,
        in_specs=[pl.BlockSpec(memory_space=vmem)]
        + [pl.BlockSpec(memory_space=smem)] * 3
        + [pl.BlockSpec(memory_space=pl.ANY)] * 2,
        out_specs=[pl.BlockSpec(memory_space=vmem)] * 2,
        scratch_shapes=[
            vmem(left_ops.shape, F32),
            vmem(left_ops.shape, F32),
            vmem((pairs * size, size), BF16),
            vmem((pairs * size, size), BF16),
            vmem((CHUNKS, 2 * width, pairs * size), BF16),
            vmem((size, pairs * size), BF16),
            vmem((size, pairs * size), BF16),
            vmem((PARTS, sec_local) + tile, F32),
            vmem((PARTS, sec_local) + tile, F32),
            vmem((PARTS, blocks) + tile, F32),
            vmem((CHUNKS, blocks, rows, width), F32),
            vmem((CHUNKS, blocks, rows, width), F32),
            vmem((PARTS, blocks) + tile, F32),
            vmem((blocks + 1,) + tile, F32),
            vmem((PARTS, places, sec_local) + tile, F32),
            vmem((2, PARTS, places, sec_local) + tile, F32),
            vmem((PARTS, places, sec_local) + tile, F32),
            vmem((2, 2, SLOTS, PARTS, sec_local) + tile, F32),
            smem((blocks,), jnp.int32),
            smem((sectors,), jnp.int32),
            pltpu.SemaphoreType.DMA((2,)),
            pltpu.SemaphoreType.DMA((PARTS,)),
            pltpu.SemaphoreType.DMA((PARTS,)),
            pltpu.SemaphoreType.DMA((PARTS,)),
            pltpu.SemaphoreType.DMA((PARTS,)),
            pltpu.SemaphoreType.DMA((PARTS,)),
            pltpu.SemaphoreType.DMA((2, PARTS)),
            pltpu.SemaphoreType.DMA((PARTS,)),
            pltpu.SemaphoreType.DMA((2, 2, SLOTS, PARTS)),
        ],
        compiler_params=pltpu.CompilerParams(
            collective_id=0, has_side_effects=True, vmem_limit_bytes=56 * 1024 * 1024
        ),
        cost_estimate=pl.CostEstimate(
            flops=flops, bytes_accessed=8 * left_ops.size, transcendentals=0
        ),
    )(theta, counts, pair_source, pair_target, left_ops, right_ops)


def solution(mesh):
    in_specs = (
        P("sec", "op", None),
        P("sec"),
        P("sec"),
        P("sec"),
        P(("sec", "op"), None, None),
        P(("sec", "op"), None, None),
    )
    out_specs = (P("sec", "op", None), P("sec", "op", None))
    return jax.shard_map(
        per_device, mesh=mesh, in_specs=in_specs, out_specs=out_specs, check_vma=False
    )
```

```python
import functools
import math

import jax
import jax.numpy as jnp
from jax import lax
from jax.experimental import pallas as pl
from jax.experimental.pallas import tpu as pltpu
from jax.sharding import PartitionSpec as P

STEPS = 3
CHUNKS = 4
CUTS = 2
PARTS = CHUNKS * CUTS
SLOTS = 4
PACE = 1
FIRST_AT, HUB_AT, FINISH_AT = 1, 4, 7
MESH = pl.DeviceIdType.MESH
F32 = jnp.float32
BF16 = jnp.bfloat16
NT = (((1,), (1,)), ((), ()))


def split(value):
    high = value.astype(BF16)
    return high, (value - high.astype(F32)).astype(BF16)


def kernel(
    factor,
    theta, counts, source, target, left, right,
    last_out, prev_out,
    left_raw, right_raw, left_hi, left_lo, right_two, x_hi, x_lo,
    current, previous, chosen, gathered, terms, arrived, running,
    pass_out, pass_in, sums, sums_in,
    before, final,
    load_sem, gather_send, gather_recv, rows_send, rows_recv,
    pass_send, pass_recv, sums_send, sums_recv,
):
    sec, op = lax.axis_index("sec"), lax.axis_index("op")
    z, core = sec // 2, sec % 2
    op_x, op_y = op // 4, op % 4
    size = left.shape[1]
    pairs = left.shape[0]
    width = size // CHUNKS
    rows = theta.shape[1]
    cut = rows // CUTS
    blocks = target.shape[0]
    sectors = final.shape[0]

    load_left = pltpu.make_async_copy(left, left_raw, load_sem.at[0])
    load_right = pltpu.make_async_copy(right, right_raw, load_sem.at[1])
    load_left.start()
    load_right.start()

    peer_x = [((op_x + k) % 4) * 4 for k in range(4)]
    peer_y = [(op_y + k) % 4 for k in range(4)]

    far_first = sorted(range(1, blocks), key=lambda k: -(min(k // 4, 4 - k // 4) + min(k % 4, 4 - k % 4)))

    def op_peer(k):
        return peer_x[k // 4] + peer_y[k % 4]

    barrier = pltpu.get_barrier_semaphore()

    for k in range(1, blocks):
        pl.semaphore_signal(barrier, 1, device_id=(sec, op_peer(k)), device_id_type=MESH)

    pl.semaphore_signal(barrier, 1, device_id=(z * 2 + (core + 1) % 2, op), device_id_type=MESH)
    for away in (1, 2, 6, 7):
        other = ((z + away) % 8) * 2 + core
        pl.semaphore_signal(barrier, 1, device_id=(other, op), device_id_type=MESH)

    def place(e):
        return e // CUTS, pl.ds(pl.multiple_of((e % CUTS) * cut, cut), cut)

    def live(h, e):
        row = lax.broadcasted_iota(jnp.int32, (cut, width), 0) + (op * rows + (e % CUTS) * cut)
        column = lax.broadcasted_iota(jnp.int32, (cut, width), 1) + (e // CUTS) * width
        return (row < counts[h]) & (column < counts[h])

    def gather_start(e):
        c, part = place(e)
        first, second = current[e, 0], current[e, 1]
        for j in range(blocks):
            chosen[e, j] = jnp.where(source[j] == 0, first, second)
        pltpu.make_async_copy(chosen.at[e, op], gathered.at[c, op, part], gather_recv.at[e]).start()

        for k in far_first:
            peer = op_peer(k)
            pltpu.make_async_remote_copy(
                chosen.at[e, peer], gathered.at[c, op, part], gather_send.at[e], gather_recv.at[e],
                device_id=(sec, peer), device_id_type=MESH,
            ).start()

    def wait_for(ref, sem):
        pltpu.make_async_copy(ref, ref, sem).wait()

    for e in range(PARTS):
        c, r = e // CUTS, (e % CUTS) * cut
        for h in range(2):
            piece = theta[h, r : r + cut, c * width : (c + 1) * width]
            current[e, h] = jnp.where(live(h, e), piece, 0.0)
    previous[...] = jnp.zeros_like(previous)
    running[blocks] = jnp.zeros((cut, width), F32)

    pl.semaphore_wait(barrier, blocks - 1 + 5)

    @pl.loop(0, PARTS)
    def _(e):
        gather_start(e)

    for b in range(blocks):
        found = jnp.int32(blocks)
        for a in range(b):
            found = jnp.where(target[a] == target[b], a, found)
        before[b] = found

    @pl.loop(0, sectors)
    def _(q):
        found = jnp.int32(blocks)
        for b in range(blocks):
            found = jnp.where(target[b] == q, b, found)
        final[q] = found

    load_left.wait()

    @pl.loop(0, pairs * size // 128)
    def _(i):
        p, r = i // (size // 128), pl.multiple_of((i % (size // 128)) * 128, 128)
        at = pl.multiple_of(i * 128, 128)
        high, low = split(left_raw[p, pl.ds(r, 128), :])
        left_hi[pl.ds(at, 128), :] = high
        left_lo[pl.ds(at, 128), :] = low

    load_right.wait()

    @pl.loop(0, CHUNKS)
    def _(c):
        for p in range(pairs):
            high, low = split(right_raw[p, pl.ds(pl.multiple_of(c * width, width), width), :])
            for d in range(CHUNKS):
                at = (d * pairs + p) * width
                right_two[c, 0:width, at : at + width] = high[:, d * width : (d + 1) * width]
                right_two[c, width : 2 * width, at : at + width] = low[:, d * width : (d + 1) * width]

    def rows_start(e):
        c, part = place(e)
        pltpu.make_async_copy(terms.at[c, op, part], arrived.at[e, op], rows_recv.at[e]).start()

        for k in far_first:
            peer = op_peer(k)
            pltpu.make_async_remote_copy(
                terms.at[c, peer, part], arrived.at[e, op], rows_send.at[e], rows_recv.at[e],
                device_id=(sec, peer), device_id_type=MESH,
            ).start()

    def away(side, distance):
        return (z + distance + side * (8 - 2 * distance)) % 8

    def sums_start(side, h, e, slot, dest, distance):
        pltpu.make_async_remote_copy(
            sums.at[e, away(side, dest)], sums_in.at[h, side, slot, e], sums_send.at[e],
            sums_recv.at[h, side, slot, e],
            device_id=(away(side, distance) * 2 + core, op), device_id_type=MESH,
        ).start()

    def sums_wait(side, h, slot, e):
        wait_for(sums_in.at[h, side, slot, e], sums_recv.at[h, side, slot, e])

    def step(k):
        half = k % 2

        def left_product(c):
            for r in range(CUTS):
                e = c * CUTS + r
                wait_for(chosen.at[e], gather_recv.at[e])
            high, low = split(gathered[c].reshape(size, width))
            both = jnp.concatenate([high, low], axis=1)

            @pl.loop(0, pairs)
            def _(p):
                at = pl.multiple_of(p * size, size)
                a = jnp.dot(left_hi[pl.ds(at, size), :], both, preferred_element_type=F32)
                b = jnp.dot(left_lo[pl.ds(at, size), :], high, preferred_element_type=F32)
                x_high, x_low = split(a[:, :width] + a[:, width:] + b)
                lane = pl.multiple_of((c * pairs + p) * width, width)
                x_hi[:, pl.ds(lane, width)] = x_high
                x_lo[:, pl.ds(lane, width)] = x_low

        def right_product(c, first, last, add):
            k_at = slice(first * pairs * width, last * pairs * width)
            for part in range(2):
                r = slice(part * (size // 2), (part + 1) * (size // 2))
                to = slice(part * (blocks // 2), (part + 1) * (blocks // 2))
                a = lax.dot_general(
                    x_hi[r, k_at], right_two[c, :, k_at], NT, preferred_element_type=F32
                )
                b = lax.dot_general(
                    x_lo[r, k_at], right_two[c, 0:width, k_at], NT, preferred_element_type=F32
                )
                block_rows = (a[:, :width] + a[:, width:] + b).reshape(blocks // 2, rows, width)
                terms[c, to] = terms[c, to] + block_rows if add else block_rows

        pl.loop(0, CHUNKS - 1)(left_product)
        right_product(0, 0, CHUNKS - 1, False)
        left_product(CHUNKS - 1)
        right_product(0, CHUNKS - 1, CHUNKS, True)
        for r in range(CUTS):
            rows_start(r)

        @pl.loop(0, PARTS)
        def _(e):
            wait_for(chosen.at[e, 0 : blocks - 1], gather_send.at[e])

        @pl.loop(1, CHUNKS)
        def _(c):
            right_product(c, 0, CHUNKS, False)
            for r in range(CUTS):
                rows_start(c * CUTS + r)

        def sum_blocks(e):
            wait_for(arrived.at[e], rows_recv.at[e])
            for b in range(blocks):
                running[b] = arrived[e, b] + running[before[b]]
            for there in range(8):
                for h in range(2):
                    pass_out[e, there, h] = running[final[4 * there + 2 * (1 - core) + h]]
            pltpu.make_async_remote_copy(
                pass_out.at[e], pass_in.at[half, e], pass_send.at[e], pass_recv.at[half, e],
                device_id=(z * 2 + (core + 1) % 2, op), device_id_type=MESH,
            ).start()
            for there in range(8):
                for h in range(2):
                    sums[e, there, h] = running[final[4 * there + 2 * core + h]]

        def sums_first(e):
            wait_for(pass_in.at[half, e], pass_recv.at[half, e])
            sums[e] = sums[e] + pass_in[half, e]
            sums_start(e % 2, half, e, 1, 4, 2)
            for side in range(2):
                sums_start(side, half, e, 0, 3, 1)
            for side in range(2):
                sums_start(side, half, e, 2, 1, 1)

        def sums_hub(e):
            for far in range(2):
                side = (e + 1 + far) % 2
                dest = away(side, 2)
                sums_wait(side, half, 0, e)
                total = sums[e, dest] + sums_in[half, side, 0, e]
                if far:
                    sums_wait(side, half, 1, e)
                    total = total + sums_in[half, side, 1, e]
                sums[e, dest] = total
                sums_start(side, half, e, 3, 2, 2)

        def finish(e):
            for side in range(2):
                sums_wait(side, half, 2, e)
                sums_wait(side, half, 3, e)
            scale = jnp.where(k == 0, factor, 2.0 * factor).astype(F32)
            keep = jnp.where(k == 0, 0.0, 1.0).astype(F32)
            for h in range(2):
                near = sums_in[half, 0, 2, e, h] + sums_in[half, 1, 2, e, h]
                far = sums_in[half, 0, 3, e, h] + sums_in[half, 1, 3, e, h]
                total = sums[e, z, h] + (near + far)
                following = jnp.where(live(h, e), scale * total, 0.0) - keep * previous[e, h]
                previous[e, h] = current[e, h]
                current[e, h] = following

            @pl.when(k < STEPS - 1)
            def _():
                gather_start(e)

        @pl.loop(0, (PARTS - 1) * PACE + FINISH_AT + 1)
        def _(t):
            def due(after, stage):
                wave = t - after
                e = wave // PACE

                @pl.when((wave >= 0) & (e < PARTS) & (wave % PACE == 0))
                def _():
                    stage(e)

            due(FINISH_AT, finish)
            due(HUB_AT, sums_hub)
            due(FIRST_AT, sums_first)
            due(0, sum_blocks)

        @pl.loop(0, PARTS)
        def _(e):
            wait_for(arrived.at[e, 0 : blocks - 1], rows_send.at[e])
            wait_for(pass_out.at[e], pass_send.at[e])
            wait_for(sums.at[e, 0:7], sums_send.at[e])

    pl.loop(0, STEPS)(step)

    for e in range(PARTS):
        c, r = e // CUTS, (e % CUTS) * cut
        for h in range(2):
            last_out[h, r : r + cut, c * width : (c + 1) * width] = current[e, h]
            prev_out[h, r : r + cut, c * width : (c + 1) * width] = previous[e, h]


def hand_over(last, prev, last_out, prev_out):
    last_out[...] = last[...]
    prev_out[...] = prev[...]


def per_device(theta, counts, pair_source, pair_target, left_ops, right_ops):
    sec_local, rows, size = theta.shape
    pairs = left_ops.shape[0]
    blocks = pair_target.shape[0]
    sectors = sec_local * lax.axis_size("sec")
    places = sectors // (2 * sec_local)
    factor = 0.5 / math.sqrt(blocks * pairs / sec_local)
    width = size // CHUNKS
    vmem, smem = pltpu.VMEM, pltpu.SMEM
    tile = (rows // CUTS, width)
    flops = STEPS * pairs * 2 * 2 * 3 * size**3
    last, prev = pl.pallas_call(
        functools.partial(kernel, factor),
        out_shape=[jax.ShapeDtypeStruct(theta.shape, F32)] * 2,
        in_specs=[pl.BlockSpec(memory_space=vmem)]
        + [pl.BlockSpec(memory_space=smem)] * 3
        + [pl.BlockSpec(memory_space=pl.ANY)] * 2,
        out_specs=[pl.BlockSpec(memory_space=vmem)] * 2,
        scratch_shapes=[
            vmem(left_ops.shape, F32),
            vmem(left_ops.shape, F32),
            vmem((pairs * size, size), BF16),
            vmem((pairs * size, size), BF16),
            vmem((CHUNKS, 2 * width, pairs * size), BF16),
            vmem((size, pairs * size), BF16),
            vmem((size, pairs * size), BF16),
            vmem((PARTS, sec_local) + tile, F32),
            vmem((PARTS, sec_local) + tile, F32),
            vmem((PARTS, blocks) + tile, F32),
            vmem((CHUNKS, blocks, rows, width), F32),
            vmem((CHUNKS, blocks, rows, width), F32),
            vmem((PARTS, blocks) + tile, F32),
            vmem((blocks + 1,) + tile, F32),
            vmem((PARTS, places, sec_local) + tile, F32),
            vmem((2, PARTS, places, sec_local) + tile, F32),
            vmem((PARTS, places, sec_local) + tile, F32),
            vmem((2, 2, SLOTS, PARTS, sec_local) + tile, F32),
            smem((blocks,), jnp.int32),
            smem((sectors,), jnp.int32),
            pltpu.SemaphoreType.DMA((2,)),
            pltpu.SemaphoreType.DMA((PARTS,)),
            pltpu.SemaphoreType.DMA((PARTS,)),
            pltpu.SemaphoreType.DMA((PARTS,)),
            pltpu.SemaphoreType.DMA((PARTS,)),
            pltpu.SemaphoreType.DMA((PARTS,)),
            pltpu.SemaphoreType.DMA((2, PARTS)),
            pltpu.SemaphoreType.DMA((PARTS,)),
            pltpu.SemaphoreType.DMA((2, 2, SLOTS, PARTS)),
        ],
        compiler_params=pltpu.CompilerParams(
            collective_id=0, has_side_effects=True, vmem_limit_bytes=56 * 1024 * 1024
        ),
        cost_estimate=pl.CostEstimate(
            flops=flops, bytes_accessed=8 * left_ops.size, transcendentals=0
        ),
    )(theta, counts, pair_source, pair_target, left_ops, right_ops)
    return pl.pallas_call(
        hand_over,
        out_shape=[jax.ShapeDtypeStruct(theta.shape, F32)] * 2,
        in_specs=[pl.BlockSpec(memory_space=vmem)] * 2,
        out_specs=[pl.BlockSpec(memory_space=vmem)] * 2,
    )(last, prev)


def solution(mesh):
    in_specs = (
        P("sec", "op", None),
        P("sec"),
        P("sec"),
        P("sec"),
        P(("sec", "op"), None, None),
        P(("sec", "op"), None, None),
    )
    out_specs = (P("sec", "op", None), P("sec", "op", None))
    return jax.shard_map(
        per_device, mesh=mesh, in_specs=in_specs, out_specs=out_specs, check_vma=False
    )
```

```python
import functools
import math

import jax
import jax.numpy as jnp
from jax import lax
from jax.experimental import pallas as pl
from jax.experimental.pallas import tpu as pltpu
from jax.sharding import PartitionSpec as P

STEPS = 3
CHUNKS = 4
CUTS = 2
PARTS = CHUNKS * CUTS
SLOTS = 4
PACE = 1
FIRST_AT, HUB_AT, FINISH_AT = 1, 4, 7
MESH = pl.DeviceIdType.MESH
F32 = jnp.float32
BF16 = jnp.bfloat16
NT = (((1,), (1,)), ((), ()))


def split(value):
    high = value.astype(BF16)
    return high, (value - high.astype(F32)).astype(BF16)


def kernel(
    factor,
    theta, counts, source, target, left, right,
    last_out, prev_out,
    left_raw, right_raw, left_hi, left_lo, right_two, x_hi, x_lo,
    current, previous, chosen, gathered, terms, arrived, running,
    pass_out, pass_in, sums, sums_in,
    before, final,
    load_sem, gather_send, gather_recv, rows_send, rows_recv,
    pass_send, pass_recv, sums_send, sums_recv,
):
    sec, op = lax.axis_index("sec"), lax.axis_index("op")
    z, core = sec // 2, sec % 2
    op_x, op_y = op // 4, op % 4
    size = left.shape[1]
    pairs = left.shape[0]
    width = size // CHUNKS
    rows = theta.shape[1]
    cut = rows // CUTS
    blocks = target.shape[0]
    sectors = final.shape[0]

    load_left = pltpu.make_async_copy(left, left_raw, load_sem.at[0])
    load_right = pltpu.make_async_copy(right, right_raw, load_sem.at[1])
    load_left.start()
    load_right.start()

    peer_x = [((op_x + k) % 4) * 4 for k in range(4)]
    peer_y = [(op_y + k) % 4 for k in range(4)]

    far_first = sorted(range(1, blocks), key=lambda k: -(min(k // 4, 4 - k // 4) + min(k % 4, 4 - k % 4)))

    def op_peer(k):
        return peer_x[k // 4] + peer_y[k % 4]

    barrier = pltpu.get_barrier_semaphore()

    for k in range(1, blocks):
        pl.semaphore_signal(barrier, 1, device_id=(sec, op_peer(k)), device_id_type=MESH)

    pl.semaphore_signal(barrier, 1, device_id=(z * 2 + (core + 1) % 2, op), device_id_type=MESH)
    for away in (1, 2, 6, 7):
        other = ((z + away) % 8) * 2 + core
        pl.semaphore_signal(barrier, 1, device_id=(other, op), device_id_type=MESH)

    def place(e):
        return e // CUTS, pl.ds(pl.multiple_of((e % CUTS) * cut, cut), cut)

    def live(h, e):
        row = lax.broadcasted_iota(jnp.int32, (cut, width), 0) + (op * rows + (e % CUTS) * cut)
        column = lax.broadcasted_iota(jnp.int32, (cut, width), 1) + (e // CUTS) * width
        return (row < counts[h]) & (column < counts[h])

    def gather_start(e):
        c, part = place(e)
        first, second = current[e, 0], current[e, 1]
        for j in range(blocks):
            chosen[e, j] = jnp.where(source[j] == 0, first, second)
        pltpu.make_async_copy(chosen.at[e, op], gathered.at[c, op, part], gather_recv.at[e]).start()

        for k in far_first:
            peer = op_peer(k)
            pltpu.make_async_remote_copy(
                chosen.at[e, peer], gathered.at[c, op, part], gather_send.at[e], gather_recv.at[e],
                device_id=(sec, peer), device_id_type=MESH,
            ).start()

    def wait_for(ref, sem):
        pltpu.make_async_copy(ref, ref, sem).wait()

    for e in range(PARTS):
        c, r = e // CUTS, (e % CUTS) * cut
        for h in range(2):
            piece = theta[h, r : r + cut, c * width : (c + 1) * width]
            current[e, h] = jnp.where(live(h, e), piece, 0.0)
    previous[...] = jnp.zeros_like(previous)
    running[blocks] = jnp.zeros((cut, width), F32)

    pl.semaphore_wait(barrier, blocks - 1 + 5)

    @pl.loop(0, PARTS)
    def _(e):
        gather_start(e)

    for b in range(blocks):
        found = jnp.int32(blocks)
        for a in range(b):
            found = jnp.where(target[a] == target[b], a, found)
        before[b] = found

    @pl.loop(0, sectors)
    def _(q):
        found = jnp.int32(blocks)
        for b in range(blocks):
            found = jnp.where(target[b] == q, b, found)
        final[q] = found

    load_left.wait()

    @pl.loop(0, pairs * size // 128)
    def _(i):
        p, r = i // (size // 128), pl.multiple_of((i % (size // 128)) * 128, 128)
        at = pl.multiple_of(i * 128, 128)
        high, low = split(left_raw[p, pl.ds(r, 128), :])
        left_hi[pl.ds(at, 128), :] = high
        left_lo[pl.ds(at, 128), :] = low

    load_right.wait()

    @pl.loop(0, CHUNKS)
    def _(c):
        for p in range(pairs):
            high, low = split(right_raw[p, pl.ds(pl.multiple_of(c * width, width), width), :])
            for d in range(CHUNKS):
                at = (d * pairs + p) * width
                right_two[c, 0:width, at : at + width] = high[:, d * width : (d + 1) * width]
                right_two[c, width : 2 * width, at : at + width] = low[:, d * width : (d + 1) * width]

    def rows_start(e):
        c, part = place(e)
        pltpu.make_async_copy(terms.at[c, op, part], arrived.at[e, op], rows_recv.at[e]).start()

        for k in far_first:
            peer = op_peer(k)
            pltpu.make_async_remote_copy(
                terms.at[c, peer, part], arrived.at[e, op], rows_send.at[e], rows_recv.at[e],
                device_id=(sec, peer), device_id_type=MESH,
            ).start()

    def away(side, distance):
        return (z + distance + side * (8 - 2 * distance)) % 8

    def sums_start(side, h, e, slot, dest, distance):
        pltpu.make_async_remote_copy(
            sums.at[e, away(side, dest)], sums_in.at[h, side, slot, e], sums_send.at[e],
            sums_recv.at[h, side, slot, e],
            device_id=(away(side, distance) * 2 + core, op), device_id_type=MESH,
        ).start()

    def sums_wait(side, h, slot, e):
        wait_for(sums_in.at[h, side, slot, e], sums_recv.at[h, side, slot, e])

    def step(k):
        half = k % 2

        def left_product(c):
            for r in range(CUTS):
                e = c * CUTS + r
                wait_for(chosen.at[e], gather_recv.at[e])
            high, low = split(gathered[c].reshape(size, width))
            both = jnp.concatenate([high, low], axis=1)

            for p in range(pairs):
                at = p * size
                a = jnp.dot(left_hi[pl.ds(at, size), :], both, preferred_element_type=F32)
                b = jnp.dot(left_lo[pl.ds(at, size), :], high, preferred_element_type=F32)
                x_high, x_low = split(a[:, :width] + a[:, width:] + b)
                lane = pl.multiple_of((c * pairs + p) * width, width)
                x_hi[:, pl.ds(lane, width)] = x_high
                x_lo[:, pl.ds(lane, width)] = x_low

        def right_product(c, first, last, add):
            k_at = slice(first * pairs * width, last * pairs * width)
            for part in range(2):
                r = slice(part * (size // 2), (part + 1) * (size // 2))
                to = slice(part * (blocks // 2), (part + 1) * (blocks // 2))
                a = lax.dot_general(
                    x_hi[r, k_at], right_two[c, :, k_at], NT, preferred_element_type=F32
                )
                b = lax.dot_general(
                    x_lo[r, k_at], right_two[c, 0:width, k_at], NT, preferred_element_type=F32
                )
                block_rows = (a[:, :width] + a[:, width:] + b).reshape(blocks // 2, rows, width)
                terms[c, to] = terms[c, to] + block_rows if add else block_rows

        pl.loop(0, CHUNKS - 1)(left_product)
        right_product(0, 0, CHUNKS - 1, False)
        left_product(CHUNKS - 1)
        right_product(0, CHUNKS - 1, CHUNKS, True)
        for r in range(CUTS):
            rows_start(r)

        @pl.loop(0, PARTS)
        def _(e):
            wait_for(chosen.at[e, 0 : blocks - 1], gather_send.at[e])

        @pl.loop(1, CHUNKS)
        def _(c):
            right_product(c, 0, CHUNKS, False)
            for r in range(CUTS):
                rows_start(c * CUTS + r)

        def sum_blocks(e):
            wait_for(arrived.at[e], rows_recv.at[e])
            for b in range(blocks):
                running[b] = arrived[e, b] + running[before[b]]
            for there in range(8):
                for h in range(2):
                    pass_out[e, there, h] = running[final[4 * there + 2 * (1 - core) + h]]
            pltpu.make_async_remote_copy(
                pass_out.at[e], pass_in.at[half, e], pass_send.at[e], pass_recv.at[half, e],
                device_id=(z * 2 + (core + 1) % 2, op), device_id_type=MESH,
            ).start()
            for there in range(8):
                for h in range(2):
                    sums[e, there, h] = running[final[4 * there + 2 * core + h]]

        def sums_first(e):
            wait_for(pass_in.at[half, e], pass_recv.at[half, e])
            sums[e] = sums[e] + pass_in[half, e]
            sums_start(e % 2, half, e, 1, 4, 2)
            for side in range(2):
                sums_start(side, half, e, 0, 3, 1)
            for side in range(2):
                sums_start(side, half, e, 2, 1, 1)

        def sums_hub(e):
            for far in range(2):
                side = (e + 1 + far) % 2
                dest = away(side, 2)
                sums_wait(side, half, 0, e)
                total = sums[e, dest] + sums_in[half, side, 0, e]
                if far:
                    sums_wait(side, half, 1, e)
                    total = total + sums_in[half, side, 1, e]
                sums[e, dest] = total
                sums_start(side, half, e, 3, 2, 2)

        def finish(e):
            for side in range(2):
                sums_wait(side, half, 2, e)
                sums_wait(side, half, 3, e)
            scale = jnp.where(k == 0, factor, 2.0 * factor).astype(F32)
            keep = jnp.where(k == 0, 0.0, 1.0).astype(F32)
            for h in range(2):
                near = sums_in[half, 0, 2, e, h] + sums_in[half, 1, 2, e, h]
                far = sums_in[half, 0, 3, e, h] + sums_in[half, 1, 3, e, h]
                total = sums[e, z, h] + (near + far)
                following = jnp.where(live(h, e), scale * total, 0.0) - keep * previous[e, h]
                previous[e, h] = current[e, h]
                current[e, h] = following

            @pl.when(k < STEPS - 1)
            def _():
                gather_start(e)

        @pl.loop(0, (PARTS - 1) * PACE + FINISH_AT + 1)
        def _(t):
            def due(after, stage):
                wave = t - after
                e = wave // PACE

                @pl.when((wave >= 0) & (e < PARTS) & (wave % PACE == 0))
                def _():
                    stage(e)

            due(FINISH_AT, finish)
            due(HUB_AT, sums_hub)
            due(FIRST_AT, sums_first)
            due(0, sum_blocks)

        @pl.loop(0, PARTS)
        def _(e):
            wait_for(arrived.at[e, 0 : blocks - 1], rows_send.at[e])
            wait_for(pass_out.at[e], pass_send.at[e])
            wait_for(sums.at[e, 0:7], sums_send.at[e])

    pl.loop(0, STEPS)(step)

    for e in range(PARTS):
        c, r = e // CUTS, (e % CUTS) * cut
        for h in range(2):
            last_out[h, r : r + cut, c * width : (c + 1) * width] = current[e, h]
            prev_out[h, r : r + cut, c * width : (c + 1) * width] = previous[e, h]


def hand_over(last, prev, last_out, prev_out):
    last_out[...] = last[...]
    prev_out[...] = prev[...]


def per_device(theta, counts, pair_source, pair_target, left_ops, right_ops):
    sec_local, rows, size = theta.shape
    pairs = left_ops.shape[0]
    blocks = pair_target.shape[0]
    sectors = sec_local * lax.axis_size("sec")
    places = sectors // (2 * sec_local)
    factor = 0.5 / math.sqrt(blocks * pairs / sec_local)
    width = size // CHUNKS
    vmem, smem = pltpu.VMEM, pltpu.SMEM
    tile = (rows // CUTS, width)
    flops = STEPS * pairs * 2 * 2 * 3 * size**3
    last, prev = pl.pallas_call(
        functools.partial(kernel, factor),
        out_shape=[jax.ShapeDtypeStruct(theta.shape, F32)] * 2,
        in_specs=[pl.BlockSpec(memory_space=vmem)]
        + [pl.BlockSpec(memory_space=smem)] * 3
        + [pl.BlockSpec(memory_space=pl.ANY)] * 2,
        out_specs=[pl.BlockSpec(memory_space=vmem)] * 2,
        scratch_shapes=[
            vmem(left_ops.shape, F32),
            vmem(left_ops.shape, F32),
            vmem((pairs * size, size), BF16),
            vmem((pairs * size, size), BF16),
            vmem((CHUNKS, 2 * width, pairs * size), BF16),
            vmem((size, pairs * size), BF16),
            vmem((size, pairs * size), BF16),
            vmem((PARTS, sec_local) + tile, F32),
            vmem((PARTS, sec_local) + tile, F32),
            vmem((PARTS, blocks) + tile, F32),
            vmem((CHUNKS, blocks, rows, width), F32),
            vmem((CHUNKS, blocks, rows, width), F32),
            vmem((PARTS, blocks) + tile, F32),
            vmem((blocks + 1,) + tile, F32),
            vmem((PARTS, places, sec_local) + tile, F32),
            vmem((2, PARTS, places, sec_local) + tile, F32),
            vmem((PARTS, places, sec_local) + tile, F32),
            vmem((2, 2, SLOTS, PARTS, sec_local) + tile, F32),
            smem((blocks,), jnp.int32),
            smem((sectors,), jnp.int32),
            pltpu.SemaphoreType.DMA((2,)),
            pltpu.SemaphoreType.DMA((PARTS,)),
            pltpu.SemaphoreType.DMA((PARTS,)),
            pltpu.SemaphoreType.DMA((PARTS,)),
            pltpu.SemaphoreType.DMA((PARTS,)),
            pltpu.SemaphoreType.DMA((PARTS,)),
            pltpu.SemaphoreType.DMA((2, PARTS)),
            pltpu.SemaphoreType.DMA((PARTS,)),
            pltpu.SemaphoreType.DMA((2, 2, SLOTS, PARTS)),
        ],
        compiler_params=pltpu.CompilerParams(
            collective_id=0, has_side_effects=True, vmem_limit_bytes=56 * 1024 * 1024
        ),
        cost_estimate=pl.CostEstimate(
            flops=flops, bytes_accessed=8 * left_ops.size, transcendentals=0
        ),
    )(theta, counts, pair_source, pair_target, left_ops, right_ops)
    return pl.pallas_call(
        hand_over,
        out_shape=[jax.ShapeDtypeStruct(theta.shape, F32)] * 2,
        in_specs=[pl.BlockSpec(memory_space=vmem)] * 2,
        out_specs=[pl.BlockSpec(memory_space=vmem)] * 2,
    )(last, prev)


def solution(mesh):
    in_specs = (
        P("sec", "op", None),
        P("sec"),
        P("sec"),
        P("sec"),
        P(("sec", "op"), None, None),
        P(("sec", "op"), None, None),
    )
    out_specs = (P("sec", "op", None), P("sec", "op", None))
    return jax.shard_map(
        per_device, mesh=mesh, in_specs=in_specs, out_specs=out_specs, check_vma=False
    )
```

```python
import functools
import math

import jax
import jax.numpy as jnp
from jax import lax
from jax.experimental import pallas as pl
from jax.experimental.pallas import tpu as pltpu
from jax.sharding import PartitionSpec as P

STEPS = 3
CHUNKS = 4
CUTS = 2
PARTS = CHUNKS * CUTS
SLOTS = 4
PACE = 1
FIRST_AT, HUB_AT, FINISH_AT = 1, 4, 7
MESH = pl.DeviceIdType.MESH
F32 = jnp.float32
BF16 = jnp.bfloat16
NT = (((1,), (1,)), ((), ()))


def split(value):
    high = value.astype(BF16)
    return high, (value - high.astype(F32)).astype(BF16)


def kernel(
    factor,
    theta, counts, source, target, left, right,
    last_out, prev_out,
    left_raw, right_raw, left_hi, left_lo, right_two, x_hi, x_lo,
    current, previous, chosen, gathered, terms, arrived, running,
    pass_out, pass_in, sums, sums_in,
    before, final,
    load_sem, gather_send, gather_recv, rows_send, rows_recv,
    pass_send, pass_recv, sums_send, sums_recv,
):
    sec, op = lax.axis_index("sec"), lax.axis_index("op")
    z, core = sec // 2, sec % 2
    op_x, op_y = op // 4, op % 4
    size = left.shape[1]
    pairs = left.shape[0]
    width = size // CHUNKS
    rows = theta.shape[1]
    cut = rows // CUTS
    blocks = target.shape[0]
    sectors = final.shape[0]

    load_left = pltpu.make_async_copy(left, left_raw, load_sem.at[0])
    load_right = pltpu.make_async_copy(right, right_raw, load_sem.at[1])
    load_left.start()
    load_right.start()

    peer_x = [((op_x + k) % 4) * 4 for k in range(4)]
    peer_y = [(op_y + k) % 4 for k in range(4)]

    far_first = sorted(range(1, blocks), key=lambda k: -(min(k // 4, 4 - k // 4) + min(k % 4, 4 - k % 4)))

    def op_peer(k):
        return peer_x[k // 4] + peer_y[k % 4]

    barrier = pltpu.get_barrier_semaphore()

    for k in range(1, blocks):
        pl.semaphore_signal(barrier, 1, device_id=(sec, op_peer(k)), device_id_type=MESH)

    pl.semaphore_signal(barrier, 1, device_id=(z * 2 + (core + 1) % 2, op), device_id_type=MESH)
    for away in (1, 2, 6, 7):
        other = ((z + away) % 8) * 2 + core
        pl.semaphore_signal(barrier, 1, device_id=(other, op), device_id_type=MESH)

    def place(e):
        return e // CUTS, pl.ds(pl.multiple_of((e % CUTS) * cut, cut), cut)

    def live(h, e):
        row = lax.broadcasted_iota(jnp.int32, (cut, width), 0) + (op * rows + (e % CUTS) * cut)
        column = lax.broadcasted_iota(jnp.int32, (cut, width), 1) + (e // CUTS) * width
        return (row < counts[h]) & (column < counts[h])

    def gather_start(e):
        c, part = place(e)
        first, second = current[e, 0], current[e, 1]
        for j in range(blocks):
            chosen[e, j] = jnp.where(source[j] == 0, first, second)
        pltpu.make_async_copy(chosen.at[e, op], gathered.at[c, op, part], gather_recv.at[e]).start()

        for k in far_first:
            peer = op_peer(k)
            pltpu.make_async_remote_copy(
                chosen.at[e, peer], gathered.at[c, op, part], gather_send.at[e], gather_recv.at[e],
                device_id=(sec, peer), device_id_type=MESH,
            ).start()

    def wait_for(ref, sem):
        pltpu.make_async_copy(ref, ref, sem).wait()

    for e in range(PARTS):
        c, r = e // CUTS, (e % CUTS) * cut
        for h in range(2):
            piece = theta[h, r : r + cut, c * width : (c + 1) * width]
            current[e, h] = jnp.where(live(h, e), piece, 0.0)
    previous[...] = jnp.zeros_like(previous)
    running[blocks] = jnp.zeros((cut, width), F32)

    pl.semaphore_wait(barrier, blocks - 1 + 5)

    @pl.loop(0, PARTS)
    def _(e):
        gather_start(e)

    for b in range(blocks):
        found = jnp.int32(blocks)
        for a in range(b):
            found = jnp.where(target[a] == target[b], a, found)
        before[b] = found

    @pl.loop(0, sectors)
    def _(q):
        found = jnp.int32(blocks)
        for b in range(blocks):
            found = jnp.where(target[b] == q, b, found)
        final[q] = found

    load_left.wait()

    @pl.loop(0, pairs * size // 128)
    def _(i):
        p, r = i // (size // 128), pl.multiple_of((i % (size // 128)) * 128, 128)
        at = pl.multiple_of(i * 128, 128)
        high, low = split(left_raw[p, pl.ds(r, 128), :])
        left_hi[pl.ds(at, 128), :] = high
        left_lo[pl.ds(at, 128), :] = low

    load_right.wait()

    @pl.loop(0, CHUNKS)
    def _(c):
        for p in range(pairs):
            high, low = split(right_raw[p, pl.ds(pl.multiple_of(c * width, width), width), :])
            for d in range(CHUNKS):
                at = (d * pairs + p) * width
                right_two[c, 0:width, at : at + width] = high[:, d * width : (d + 1) * width]
                right_two[c, width : 2 * width, at : at + width] = low[:, d * width : (d + 1) * width]

    def rows_start(e):
        c, part = place(e)
        pltpu.make_async_copy(terms.at[c, op, part], arrived.at[e, op], rows_recv.at[e]).start()

        for k in far_first:
            peer = op_peer(k)
            pltpu.make_async_remote_copy(
                terms.at[c, peer, part], arrived.at[e, op], rows_send.at[e], rows_recv.at[e],
                device_id=(sec, peer), device_id_type=MESH,
            ).start()

    def away(side, distance):
        return (z + distance + side * (8 - 2 * distance)) % 8

    def sums_start(side, h, e, slot, dest, distance):
        pltpu.make_async_remote_copy(
            sums.at[e, away(side, dest)], sums_in.at[h, side, slot, e], sums_send.at[e],
            sums_recv.at[h, side, slot, e],
            device_id=(away(side, distance) * 2 + core, op), device_id_type=MESH,
        ).start()

    def sums_wait(side, h, slot, e):
        wait_for(sums_in.at[h, side, slot, e], sums_recv.at[h, side, slot, e])

    def step(k):
        half = k % 2

        def left_product(c):
            for r in range(CUTS):
                e = c * CUTS + r
                wait_for(chosen.at[e], gather_recv.at[e])
            high, low = split(gathered[c].reshape(size, width))
            both = jnp.concatenate([high, low], axis=1)

            for p in range(pairs):
                at = p * size
                a = jnp.dot(left_hi[pl.ds(at, size), :], both, preferred_element_type=F32)
                b = jnp.dot(left_lo[pl.ds(at, size), :], high, preferred_element_type=F32)
                x_high, x_low = split(a[:, :width] + a[:, width:] + b)
                lane = pl.multiple_of((c * pairs + p) * width, width)
                x_hi[:, pl.ds(lane, width)] = x_high
                x_lo[:, pl.ds(lane, width)] = x_low

        def right_product(c, first, last, add):
            k_at = slice(first * pairs * width, last * pairs * width)
            for part in range(2):
                r = slice(part * (size // 2), (part + 1) * (size // 2))
                to = slice(part * (blocks // 2), (part + 1) * (blocks // 2))
                a = lax.dot_general(
                    x_hi[r, k_at], right_two[c, :, k_at], NT, preferred_element_type=F32
                )
                b = lax.dot_general(
                    x_lo[r, k_at], right_two[c, 0:width, k_at], NT, preferred_element_type=F32
                )
                block_rows = (a[:, :width] + a[:, width:] + b).reshape(blocks // 2, rows, width)
                terms[c, to] = terms[c, to] + block_rows if add else block_rows

        pl.loop(0, CHUNKS - 1)(left_product)
        right_product(0, 0, CHUNKS - 1, False)
        left_product(CHUNKS - 1)
        right_product(0, CHUNKS - 1, CHUNKS, True)
        for r in range(CUTS):
            rows_start(r)

        @pl.loop(0, PARTS)
        def _(e):
            wait_for(chosen.at[e, 0 : blocks - 1], gather_send.at[e])

        for c in range(1, CHUNKS):
            right_product(c, 0, CHUNKS, False)
            for r in range(CUTS):
                rows_start(c * CUTS + r)

        def sum_blocks(e):
            wait_for(arrived.at[e], rows_recv.at[e])
            for b in range(blocks):
                running[b] = arrived[e, b] + running[before[b]]
            for there in range(8):
                for h in range(2):
                    pass_out[e, there, h] = running[final[4 * there + 2 * (1 - core) + h]]
            pltpu.make_async_remote_copy(
                pass_out.at[e], pass_in.at[half, e], pass_send.at[e], pass_recv.at[half, e],
                device_id=(z * 2 + (core + 1) % 2, op), device_id_type=MESH,
            ).start()
            for there in range(8):
                for h in range(2):
                    sums[e, there, h] = running[final[4 * there + 2 * core + h]]

        def sums_first(e):
            wait_for(pass_in.at[half, e], pass_recv.at[half, e])
            sums[e] = sums[e] + pass_in[half, e]
            sums_start(e % 2, half, e, 1, 4, 2)
            for side in range(2):
                sums_start(side, half, e, 0, 3, 1)
            for side in range(2):
                sums_start(side, half, e, 2, 1, 1)

        def sums_hub(e):
            for far in range(2):
                side = (e + 1 + far) % 2
                dest = away(side, 2)
                sums_wait(side, half, 0, e)
                total = sums[e, dest] + sums_in[half, side, 0, e]
                if far:
                    sums_wait(side, half, 1, e)
                    total = total + sums_in[half, side, 1, e]
                sums[e, dest] = total
                sums_start(side, half, e, 3, 2, 2)

        def finish(e):
            for side in range(2):
                sums_wait(side, half, 2, e)
                sums_wait(side, half, 3, e)
            scale = jnp.where(k == 0, factor, 2.0 * factor).astype(F32)
            keep = jnp.where(k == 0, 0.0, 1.0).astype(F32)
            for h in range(2):
                near = sums_in[half, 0, 2, e, h] + sums_in[half, 1, 2, e, h]
                far = sums_in[half, 0, 3, e, h] + sums_in[half, 1, 3, e, h]
                total = sums[e, z, h] + (near + far)
                following = jnp.where(live(h, e), scale * total, 0.0) - keep * previous[e, h]
                previous[e, h] = current[e, h]
                current[e, h] = following

            @pl.when(k < STEPS - 1)
            def _():
                gather_start(e)

        @pl.loop(0, (PARTS - 1) * PACE + FINISH_AT + 1)
        def _(t):
            def due(after, stage):
                wave = t - after
                e = wave // PACE

                @pl.when((wave >= 0) & (e < PARTS) & (wave % PACE == 0))
                def _():
                    stage(e)

            due(FINISH_AT, finish)
            due(HUB_AT, sums_hub)
            due(FIRST_AT, sums_first)
            due(0, sum_blocks)

        @pl.loop(0, PARTS)
        def _(e):
            wait_for(arrived.at[e, 0 : blocks - 1], rows_send.at[e])
            wait_for(pass_out.at[e], pass_send.at[e])
            wait_for(sums.at[e, 0:7], sums_send.at[e])

    pl.loop(0, STEPS)(step)

    for e in range(PARTS):
        c, r = e // CUTS, (e % CUTS) * cut
        for h in range(2):
            last_out[h, r : r + cut, c * width : (c + 1) * width] = current[e, h]
            prev_out[h, r : r + cut, c * width : (c + 1) * width] = previous[e, h]


def hand_over(last, prev, last_out, prev_out):
    last_out[...] = last[...]
    prev_out[...] = prev[...]


def per_device(theta, counts, pair_source, pair_target, left_ops, right_ops):
    sec_local, rows, size = theta.shape
    pairs = left_ops.shape[0]
    blocks = pair_target.shape[0]
    sectors = sec_local * lax.axis_size("sec")
    places = sectors // (2 * sec_local)
    factor = 0.5 / math.sqrt(blocks * pairs / sec_local)
    width = size // CHUNKS
    vmem, smem = pltpu.VMEM, pltpu.SMEM
    tile = (rows // CUTS, width)
    flops = STEPS * pairs * 2 * 2 * 3 * size**3
    last, prev = pl.pallas_call(
        functools.partial(kernel, factor),
        out_shape=[jax.ShapeDtypeStruct(theta.shape, F32)] * 2,
        in_specs=[pl.BlockSpec(memory_space=vmem)]
        + [pl.BlockSpec(memory_space=smem)] * 3
        + [pl.BlockSpec(memory_space=pl.ANY)] * 2,
        out_specs=[pl.BlockSpec(memory_space=vmem)] * 2,
        scratch_shapes=[
            vmem(left_ops.shape, F32),
            vmem(left_ops.shape, F32),
            vmem((pairs * size, size), BF16),
            vmem((pairs * size, size), BF16),
            vmem((CHUNKS, 2 * width, pairs * size), BF16),
            vmem((size, pairs * size), BF16),
            vmem((size, pairs * size), BF16),
            vmem((PARTS, sec_local) + tile, F32),
            vmem((PARTS, sec_local) + tile, F32),
            vmem((PARTS, blocks) + tile, F32),
            vmem((CHUNKS, blocks, rows, width), F32),
            vmem((CHUNKS, blocks, rows, width), F32),
            vmem((PARTS, blocks) + tile, F32),
            vmem((blocks + 1,) + tile, F32),
            vmem((PARTS, places, sec_local) + tile, F32),
            vmem((2, PARTS, places, sec_local) + tile, F32),
            vmem((PARTS, places, sec_local) + tile, F32),
            vmem((2, 2, SLOTS, PARTS, sec_local) + tile, F32),
            smem((blocks,), jnp.int32),
            smem((sectors,), jnp.int32),
            pltpu.SemaphoreType.DMA((2,)),
            pltpu.SemaphoreType.DMA((PARTS,)),
            pltpu.SemaphoreType.DMA((PARTS,)),
            pltpu.SemaphoreType.DMA((PARTS,)),
            pltpu.SemaphoreType.DMA((PARTS,)),
            pltpu.SemaphoreType.DMA((PARTS,)),
            pltpu.SemaphoreType.DMA((2, PARTS)),
            pltpu.SemaphoreType.DMA((PARTS,)),
            pltpu.SemaphoreType.DMA((2, 2, SLOTS, PARTS)),
        ],
        compiler_params=pltpu.CompilerParams(
            collective_id=0, has_side_effects=True, vmem_limit_bytes=56 * 1024 * 1024
        ),
        cost_estimate=pl.CostEstimate(
            flops=flops, bytes_accessed=8 * left_ops.size, transcendentals=0
        ),
    )(theta, counts, pair_source, pair_target, left_ops, right_ops)
    return pl.pallas_call(
        hand_over,
        out_shape=[jax.ShapeDtypeStruct(theta.shape, F32)] * 2,
        in_specs=[pl.BlockSpec(memory_space=vmem)] * 2,
        out_specs=[pl.BlockSpec(memory_space=vmem)] * 2,
    )(last, prev)


def solution(mesh):
    in_specs = (
        P("sec", "op", None),
        P("sec"),
        P("sec"),
        P("sec"),
        P(("sec", "op"), None, None),
        P(("sec", "op"), None, None),
    )
    out_specs = (P("sec", "op", None), P("sec", "op", None))
    return jax.shard_map(
        per_device, mesh=mesh, in_specs=in_specs, out_specs=out_specs, check_vma=False
    )
```
